32 devices in a mesh: groups: 2 (over x), row: 8 (over z, y), col: 2 (over core).
Axes of the slice: x: 2, y: 2, z: 4, core: 2. Of those that a mesh axis runs over, the one named last changes fastest.
Arguments:
- density: float32 [192, 10, 128, 128], P(('groups', 'row', 'col')), parts along dimension 0, may hold values from -0.5 to 0.5
- pattern_table: int32 [64, 96, 10], replicated, may hold values from 0 to 95, as said below
- structure_id: int32 [2], P('groups'), parts along dimension 0, may hold values from 0 to 63
Outputs:
- purified: float32 [192, 10, 128, 128], P(('groups', 'row', 'col')), parts along dimension 0
The draws below stay inside these ranges and needn't reach their ends.
There are 2 independent parts, one for each index of `groups`. The reference program is written for one: setup_inputs(seed, part) draws one part's arguments, and reference() takes and returns one part's arrays. A program takes and returns all parts, laid end to end along the dimension named above; an argument that names none is the same for every part. Nothing has to cross between parts.
Inputs may be any that keep to these rules, and one draw needn't show every extreme that they name: pattern_table[s, i, 0] = i; the 10 entries of a row are distinct, and each differs from i, modulo 96, by at most 12.
All inputs are finite; a program needn't handle non-finite values.
Results may differ from the reference program's by a relative error of at most 0.0003.
Values sent between devices are 32-bit elements; how exact they have to be, the bound alone decides.
A program may use at most 128 MiB of HBM per device.

```python
import jax
import jax.numpy as jnp
from jax import lax

BS = 128
KB = 10
HOPS = 2
STRUCTS = 64
BR_DEV = 6
NB = 96


def draw_pattern_table(key, part):
    key = jax.random.fold_in(key, 7)
    reach = HOPS * BR_DEV
    keys = jax.random.split(key, STRUCTS * NB)
    offsets = jnp.concatenate([jnp.arange(1, reach + 1, dtype=jnp.int32), -jnp.arange(1, reach + 1, dtype=jnp.int32)])

    def pick_offsets(one_key):
        return jax.random.permutation(one_key, offsets)[:KB - 1]
    chosen = jax.vmap(pick_offsets)(keys).reshape(STRUCTS, NB, KB - 1)
    own_rows = jnp.arange(NB, dtype=jnp.int32)[None, :, None]
    shifts = jnp.concatenate([jnp.zeros((STRUCTS, NB, 1), jnp.int32), chosen], axis=2)
    return jnp.mod(own_rows + shifts, NB).astype(jnp.int32)


def steps_of(rng, extent, cuts, low, top_value):
    loudness, own = 1.0, jax.random.fold_in(rng, 6)
    for axis_at, blocks in cuts:
        heights = jnp.exp(jax.random.uniform(jax.random.fold_in(own, axis_at), (blocks,), jnp.float32, low / len(cuts), top_value / len(cuts)))
        loudness = loudness * jnp.repeat(heights, extent[axis_at] // blocks).reshape([-1 if axis == axis_at else 1 for axis in range(len(extent))])
    return loudness


def noise(key, extent, spread, most, cuts=(), kind=jnp.bfloat16):
    level = steps_of(key, extent, cuts, -0.22, 0.18) if cuts else 1.0
    entries = jax.random.normal(key, extent, jnp.float32) * spread * level
    return jnp.minimum(jnp.maximum(entries, -most), most).astype(kind)


def setup_inputs(seed: int = 0, part: int = 0) -> dict:
    seeds = jax.random.split(jax.random.key(seed), 4)
    part_splits = jax.random.split(jax.random.fold_in(seeds[3], part), 4)
    density = noise(part_splits[0], (NB, KB, BS, BS), BS ** -0.5, 0.5, ((0, 16),), jnp.float32)
    pattern_table = draw_pattern_table(jax.random.fold_in(seeds[3], 71), part)
    structure_id = jax.random.randint(part_splits[2], (1,), 0, STRUCTS).astype(jnp.int32)
    return dict(density=density, pattern_table=pattern_table, structure_id=structure_id)


def purify_row(window, window_first, pattern, own_blocks, global_row):
    total_rows = pattern.shape[0]
    blocks = pattern.shape[1]
    columns = lax.dynamic_index_in_dim(pattern, global_row, 0, keepdims=False).astype(jnp.int32)
    where_rows = jnp.mod(columns - window_first, total_rows).astype(jnp.int32)
    fetched = window[where_rows]
    fetched_cols = pattern[columns]
    matches = fetched_cols[:, :, None] == columns[None, None, :]
    slot_ids = jnp.arange(blocks, dtype=jnp.int32)
    chosen = jnp.sum(jnp.where(matches, slot_ids[None, :, None], 0), axis=1).astype(jnp.int32)
    present = jnp.any(matches, axis=1)
    picked = fetched[slot_ids[:, None], chosen]
    linked = jnp.where(present[:, :, None, None], picked, jnp.zeros_like(picked))
    square = jnp.einsum("axz,aczy->cxy", own_blocks, linked, precision=lax.Precision.HIGHEST)
    cube = jnp.einsum("axz,aczy->cxy", square, linked, precision=lax.Precision.HIGHEST)
    return 3.0 * square - 2.0 * cube


def reference(density, pattern_table, structure_id):
    pattern = lax.dynamic_index_in_dim(pattern_table, structure_id[0], 0, keepdims=False)

    def one_row(inputs):
        own_blocks, local_row = inputs
        return purify_row(density, jnp.int32(0), pattern, own_blocks, local_row)

    return lax.map(one_row, (density, jnp.arange(NB, dtype=jnp.int32)))
```

```python
import functools

import jax
import jax.numpy as jnp
from jax import lax
from jax.experimental import pallas as pl
from jax.experimental.pallas import tpu as pltpu
from jax.sharding import PartitionSpec as P

PIECE = 5
AHEAD = 3
LAG = 2
MESH = pl.DeviceIdType.MESH


def spread_kernel(chips, pieces, own, partner, across, onward, far,
                  p_send, p_recv, y_send, y_recv, z_send, z_recv, x_send, x_recv):
    chip = lax.axis_index("row")
    core = lax.axis_index("col")
    even = lax.rem(chip, 2) == 0
    step = jnp.where(even, 1, -1)
    paired = {"row": chip + step}
    target = {"row": lax.rem(chip + 2 * step + chips, chips)}
    source = {"row": lax.rem(chip - 2 * step + chips, chips)}
    other = {"col": 1 - core}

    barrier = pltpu.get_barrier_semaphore()
    for device in (paired, target, source, other):
        pl.semaphore_signal(barrier, inc=1, device_id=device, device_id_type=MESH)
    pl.semaphore_wait(barrier, 4)

    def copy(src, dst, send, recv, device):
        return pltpu.make_async_remote_copy(
            src_ref=src, dst_ref=dst, send_sem=send, recv_sem=recv,
            device_id=device, device_id_type=MESH)

    def part(n):
        return pl.ds(n * PIECE, PIECE)

    whole = copy(own, partner, p_send, p_recv, other)
    ys = [copy(own.at[part(n)], across.at[part(n)], y_send.at[n], y_recv.at[n], paired)
          for n in range(pieces)]
    zs = [copy(across.at[part(n)], onward.at[part(n)], z_send.at[n], z_recv.at[n], target)
          for n in range(pieces)]
    xy = [copy(across.at[part(n)], far.at[part(n)], x_send.at[n], x_recv.at[n], other)
          for n in range(pieces)]
    xz = [copy(onward.at[part(n)], far.at[part(n)], x_send.at[n], x_recv.at[n], other)
          for n in range(pieces)]
    from_across = lax.rem(chip, 2) == core

    def onward_arrived(n):
        zs[n].wait_recv()

        @pl.when(jnp.logical_not(from_across))
        def _():
            xz[n].start()

    for n in range(min(AHEAD, pieces)):
        ys[n].start()
    whole.start()
    for n in range(pieces):
        ys[n].wait_recv()
        zs[n].start()

        @pl.when(from_across)
        def _():
            xy[n].start()

        if n + AHEAD < pieces:
            ys[n].wait_send()
            ys[n + AHEAD].start()
        if n >= LAG:
            onward_arrived(n - LAG)
    for n in range(max(pieces - LAG, 0), pieces):
        onward_arrived(n)
    for n in range(pieces):
        if n + AHEAD >= pieces:
            ys[n].wait_send()
        zs[n].wait_send()
        xy[n].wait()
    whole.wait()


def spread(blocks, chips):
    pieces = blocks.shape[0] // PIECE
    dma = pltpu.SemaphoreType.DMA
    shard = jax.ShapeDtypeStruct(blocks.shape, blocks.dtype)
    return pl.pallas_call(
        functools.partial(spread_kernel, chips, pieces),
        out_shape=[shard] * 4,
        in_specs=[pl.BlockSpec(memory_space=pl.ANY)],
        out_specs=[pl.BlockSpec(memory_space=pl.ANY)] * 4,
        scratch_shapes=[dma, dma] + [dma((pieces,))] * 6,
        compiler_params=pltpu.CompilerParams(collective_id=0, has_side_effects=True),
    )(blocks)


def purify_kernel(rows, slots, where, own, partner, across, onward, far, out,
                  stage, high, low, wide, square, square_wide, sem):
    shards = (own, partner, across, onward, far)
    held = rows * slots
    half = held // 2
    width = out.shape[-1]
    jobs = [(s, h) for s in range(len(shards)) for h in range(2)]

    def load(n):
        s, h = jobs[n]
        return pltpu.make_async_copy(
            shards[s].at[pl.ds(h * half, half)], stage.at[n % 2], sem.at[n % 2])

    def halves(x):
        top = x.astype(jnp.bfloat16)
        return top, (x - top.astype(jnp.float32)).astype(jnp.bfloat16)

    load(0).start()
    high[len(shards) * held] = jnp.zeros((width, width), jnp.bfloat16)
    low[len(shards) * held] = jnp.zeros((width, width), jnp.bfloat16)
    for n in range(len(jobs)):
        if n + 1 < len(jobs):
            load(n + 1).start()
        load(n).wait()

        def split_one(b, _):
            top, rest = halves(stage[n % 2, b])
            high[n * half + b] = top
            low[n * half + b] = rest
            return 0

        lax.fori_loop(0, half, split_one, 0, unroll=2)

    def product(factor, row, c):
        tops, rests = [], []
        for a in range(slots):
            places = [where[(row * slots + a) * slots + c + k] for k in range(2)]
            tops.append(jnp.concatenate([high[p] for p in places], axis=1))
            rests.append(jnp.concatenate([low[p] for p in places], axis=1))
        both = jnp.dot(factor[...], jnp.concatenate(tops, axis=0),
                       preferred_element_type=jnp.float32)
        small = jnp.dot(factor[:width], jnp.concatenate(rests, axis=0),
                        preferred_element_type=jnp.float32)
        return both[:width] + (both[width:] + small)

    def one_row(row, _):
        for a in range(slots):
            columns = slice(a * width, (a + 1) * width)
            wide[:width, columns] = high[row * slots + a]
            wide[width:, columns] = low[row * slots + a]
        for c in range(0, slots, 2):
            columns = slice(c * width, (c + 2) * width)
            result = product(wide, row, c)
            square[:, columns] = result
            top, rest = halves(result)
            square_wide[:width, columns] = top
            square_wide[width:, columns] = rest
        for c in range(0, slots, 2):
            columns = slice(c * width, (c + 2) * width)
            result = 3.0 * square[:, columns] - 2.0 * product(square_wide, row, c)
            out[row, c] = result[:, :width]
            out[row, c + 1] = result[:, width:]
        return 0

    lax.fori_loop(0, rows, one_row, 0)


def purify(where, shards, rows, slots):
    held, width, _ = shards[0].shape
    count = len(shards) * held + 1
    vmem, narrow = pltpu.VMEM, jnp.bfloat16
    return pl.pallas_call(
        functools.partial(purify_kernel, rows, slots),
        out_shape=jax.ShapeDtypeStruct((rows, slots, width, width), jnp.float32),
        in_specs=[pl.BlockSpec(memory_space=pltpu.SMEM)]
        + [pl.BlockSpec(memory_space=pl.ANY)] * len(shards),
        out_specs=pl.BlockSpec(memory_space=vmem),
        scratch_shapes=[
            vmem((2, held // 2, width, width), jnp.float32),
            vmem((count, width, width), narrow),
            vmem((count, width, width), narrow),
            vmem((2 * width, slots * width), narrow),
            vmem((width, slots * width), jnp.float32),
            vmem((2 * width, slots * width), narrow),
            pltpu.SemaphoreType.DMA((2,)),
        ],
        compiler_params=pltpu.CompilerParams(vmem_limit_bytes=50 * 1024 * 1024),
    )(where, *shards)


def block_places(pattern, rows, chip, core):
    total, slots = pattern.shape
    first = (2 * chip + core) * rows
    own = lax.dynamic_slice_in_dim(pattern, first, rows, 0)
    fetched = pattern[own]
    matches = fetched[:, :, None, :] == own[:, None, :, None]
    slot = jnp.sum(jnp.where(matches, jnp.arange(slots, dtype=jnp.int32), 0), axis=3)
    present = jnp.any(matches, axis=3)
    frame = jnp.mod(own - (2 * chip - 2) * rows, total)
    group, local = frame // rows, frame % rows
    from_across = jnp.where(chip % 2 == 0, group >= 4, group < 2)
    shard = jnp.where(group == 2 + core, 0,
            jnp.where(group == 3 - core, 1,
            jnp.where(group == 1 + 3 * core, 4,
            jnp.where(from_across, 2, 3))))
    base = (shard * rows + local) * slots
    return jnp.where(present, base[:, :, None] + slot, 5 * rows * slots).reshape(-1)


def body(density, pattern_table, structure_id):
    rows, slots, width, _ = density.shape
    chip, core = lax.axis_index("row"), lax.axis_index("col")
    pattern = lax.dynamic_index_in_dim(pattern_table, structure_id[0], 0, keepdims=False)
    where = block_places(pattern, rows, chip, core)
    blocks = density.reshape(rows * slots, width, width)
    shards = (blocks, *spread(blocks, lax.axis_size("row")))
    return purify(where, shards, rows, slots)


def solution(mesh):
    return jax.shard_map(
        body,
        mesh=mesh,
        in_specs=(P(("groups", "row", "col"), None, None, None), P(), P("groups")),
        out_specs=P(("groups", "row", "col"), None, None, None),
        check_vma=False,
    )
```

```python
import functools

import jax
import jax.numpy as jnp
from jax import lax
from jax.experimental import pallas as pl
from jax.experimental.pallas import tpu as pltpu
from jax.sharding import PartitionSpec as P

PIECE = 5
AHEAD = 3
LAG = 2
MESH = pl.DeviceIdType.MESH
OWN, PARTNER, ACROSS, ONWARD, FAR = range(5)
SHARDS = 5


def halves(x):
    top = x.astype(jnp.bfloat16)
    return top, (x - top.astype(jnp.float32)).astype(jnp.bfloat16)


def purify_kernel(chips, total, rows, slots, pattern, own, out,
                  partner, across, onward, far, high, low, square, wide, wider,
                  linked, factor, line,
                  p_send, p_recv, y_send, y_recv, z_send, z_recv, x_send, x_recv):
    width = out.shape[-1]
    held = rows * slots
    pieces = held // PIECE
    per_row = slots // PIECE
    lines = SHARDS * rows
    nothing = SHARDS * held
    chip = lax.axis_index("row")
    core = lax.axis_index("col")
    even = lax.rem(chip, 2) == 0
    step = jnp.where(even, 1, -1)
    paired = {"row": chip + step}
    target = {"row": lax.rem(chip + 2 * step + chips, chips)}
    source = {"row": lax.rem(chip - 2 * step + chips, chips)}
    other = {"col": 1 - core}

    barrier = pltpu.get_barrier_semaphore()
    for device in (paired, target, source, other):
        pl.semaphore_signal(barrier, inc=1, device_id=device, device_id_type=MESH)
    pl.semaphore_wait(barrier, 4)

    def copy(src, dst, send, recv, device):
        return pltpu.make_async_remote_copy(
            src_ref=src, dst_ref=dst, send_sem=send, recv_sem=recv,
            device_id=device, device_id_type=MESH)

    def part(n):
        return pl.ds(n * PIECE, PIECE)

    whole = copy(own, partner, p_send, p_recv, other)
    ys = [copy(own.at[part(n)], across.at[part(n)], y_send.at[n], y_recv.at[n], paired)
          for n in range(pieces)]
    zs = [copy(across.at[part(n)], onward.at[part(n)], z_send.at[n], z_recv.at[n], target)
          for n in range(pieces)]
    xy = [copy(across.at[part(n)], far.at[part(n)], x_send.at[n], x_recv.at[n], other)
          for n in range(pieces)]
    xz = [copy(onward.at[part(n)], far.at[part(n)], x_send.at[n], x_recv.at[n], other)
          for n in range(pieces)]
    from_across = lax.rem(chip, 2) == core

    for n in range(min(AHEAD, pieces)):
        ys[n].start()
    whole.start()

    def split(ref, shard, first, count):
        def one(b, _):
            top, rest = halves(ref[first + b])
            high[shard * held + first + b] = top
            low[shard * held + first + b] = rest
            return 0

        lax.fori_loop(0, count, one, 0)

    def wrapped(x):
        x = jnp.where(x < 0, x + total, x)
        return jnp.where(x >= total, x - total, x)

    mine = (2 * chip + core) * rows
    toward = chip + step
    away = lax.rem(chip - step + chips, chips)
    side = lax.rem(chip - 1 + 2 * core + chips, chips)
    firsts = [mine, (2 * chip + 1 - core) * rows, (2 * toward + core) * rows,
              (2 * away + core) * rows, (2 * side + 1 - core) * rows]

    def tabulate(row, _):
        columns = [pattern[(mine + row) * slots + a] for a in range(slots)]
        places = []
        for a in range(slots):
            place = jnp.int32(0)
            for shard, first in enumerate(firsts):
                off = wrapped(columns[a] - first)
                place = jnp.where(off < rows, shard * rows + off, place)
            line[row * slots + a] = place
            places.append(place)

        def one_line(m, _):
            shard, local = m // rows, m % rows
            at = jnp.int32(0)
            for s, first in enumerate(firsts):
                at = jnp.where(shard == s, first, at)
            at = wrapped(at + local)
            entries = [pattern[at * slots + b] for b in range(slots)]
            slot = jnp.int32(nothing)
            for a in range(slots):
                slot = jnp.where(places[a] == m, row * slots + a, slot)
            factor[row * lines + m] = slot
            for c in range(slots):
                found = jnp.int32(nothing)
                for b in range(slots):
                    found = jnp.where(entries[b] == columns[c], m * slots + b, found)
                linked[(row * lines + m) * slots + c] = found
            return 0

        lax.fori_loop(0, lines, one_line, 0)
        return 0

    def product(left, row, which, c):
        tops, rests = [], []
        for m in which:
            places = [linked[(row * lines + m) * slots + c + k] for k in range(2)]
            tops.append(jnp.concatenate([high[p] for p in places], axis=1))
            rests.append(jnp.concatenate([low[p] for p in places], axis=1))
        both = jnp.dot(left[:, :len(which) * width], jnp.concatenate(tops, axis=0),
                       preferred_element_type=jnp.float32)
        small = jnp.dot(left[:width, :len(which) * width], jnp.concatenate(rests, axis=0),
                        preferred_element_type=jnp.float32)
        return both[:width] + (both[width:] + small)

    def add_lines(which, begin, end, fresh=False):
        def one_row(row, _):
            for t, m in enumerate(which):
                place = factor[row * lines + m]
                wide[:width, t * width:(t + 1) * width] = high[place]
                wide[width:, t * width:(t + 1) * width] = low[place]
            for c in range(0, slots, 2):
                columns = slice(c * width, (c + 2) * width)
                result = product(wide, row, which, c)
                if fresh:
                    square[row, :, columns] = result
                else:
                    square[row, :, columns] += result
            return 0

        lax.fori_loop(begin, end, one_row, 0)

    def remote_lines(r):
        return [shard * rows + r for shard in (ACROSS, ONWARD, FAR)]

    def onward_arrived(n):
        zs[n].wait_recv()

        @pl.when(jnp.logical_not(from_across))
        def _():
            xz[n].start()

        split(onward, ONWARD, n * PIECE, PIECE)

    def far_arrived(n):
        xy[n].wait_recv()
        split(far, FAR, n * PIECE, PIECE)

    middle = rows // 2
    near = list(range(2 * rows))
    jobs = {}

    def at(n, job, *args):
        jobs.setdefault(n, []).append((job, args))

    def partner_arrived():
        whole.wait_recv()
        split(partner, PARTNER, 0, held)

    def tables(begin, end):
        lax.fori_loop(begin, end, tabulate, 0)

    at(0, tables, 0, rows // 3)
    at(1, tables, rows // 3, 2 * rows // 3)
    at(2, tables, 2 * rows // 3, rows)
    at(2, partner_arrived)
    at(3, add_lines, near, 0, middle, True)
    at(4, add_lines, near, middle, rows, True)
    for r in range(rows - 1):
        ready = (r + 1) * per_row + LAG + 1
        at(ready, add_lines, remote_lines(r), 0, middle)
        at(ready + 1, add_lines, remote_lines(r), middle, rows)

    high[nothing] = jnp.zeros((width, width), jnp.bfloat16)
    low[nothing] = jnp.zeros((width, width), jnp.bfloat16)
    split(own, OWN, 0, held)
    for n in range(pieces + LAG + 1):
        if n < pieces:
            ys[n].wait_recv()
            zs[n].start()

            @pl.when(from_across)
            def _():
                xy[n].start()

            if n + AHEAD < pieces:
                ys[n].wait_send()
                ys[n + AHEAD].start()
            split(across, ACROSS, n * PIECE, PIECE)
        if LAG <= n < pieces + LAG:
            onward_arrived(n - LAG)
        if n >= LAG + 1:
            far_arrived(n - LAG - 1)
        for job, args in jobs.pop(n, []):
            job(*args)
    for n in sorted(jobs):
        for job, args in jobs[n]:
            job(*args)
    add_lines(remote_lines(rows - 1), 0, rows)

    def finish(row, _):
        for c in range(0, slots, 2):
            columns = slice(c * width, (c + 2) * width)
            top, rest = halves(square[row, :, columns])
            wider[:width, columns] = top
            wider[width:, columns] = rest
        which = [line[row * slots + a] for a in range(slots)]
        for c in range(0, slots, 2):
            columns = slice(c * width, (c + 2) * width)
            result = 3.0 * square[row, :, columns] - 2.0 * product(wider, row, which, c)
            out[row, c] = result[:, :width]
            out[row, c + 1] = result[:, width:]
        return 0

    lax.fori_loop(0, rows, finish, 0)
    for n in range(pieces):
        if n + AHEAD >= pieces:
            ys[n].wait_send()
        zs[n].wait_send()
        xy[n].wait_send()
    whole.wait_send()


def body(density, pattern_table, structure_id):
    rows, slots, width, _ = density.shape
    total = pattern_table.shape[1]
    held = rows * slots
    pieces = held // PIECE
    pattern = lax.dynamic_index_in_dim(pattern_table, structure_id[0], 0, keepdims=False)
    blocks = density.reshape(held, width, width)
    dma, vmem, smem, narrow = pltpu.SemaphoreType.DMA, pltpu.VMEM, pltpu.SMEM, jnp.bfloat16
    lines = SHARDS * rows
    return pl.pallas_call(
        functools.partial(purify_kernel, lax.axis_size("row"), total, rows, slots),
        out_shape=jax.ShapeDtypeStruct(density.shape, density.dtype),
        in_specs=[pl.BlockSpec(memory_space=smem), pl.BlockSpec(memory_space=vmem)],
        out_specs=pl.BlockSpec(memory_space=vmem),
        scratch_shapes=[vmem(blocks.shape, blocks.dtype)] * 4
        + [vmem((SHARDS * held + 1, width, width), narrow)] * 2
        + [
            vmem((rows, width, slots * width), jnp.float32),
            vmem((2 * width, 2 * rows * width), narrow),
            vmem((2 * width, slots * width), narrow),
            smem((rows * lines * slots,), jnp.int32),
            smem((rows * lines,), jnp.int32),
            smem((rows * slots,), jnp.int32),
            dma, dma,
        ] + [dma((pieces,))] * 6,
        compiler_params=pltpu.CompilerParams(
            collective_id=0, has_side_effects=True, vmem_limit_bytes=56 * 1024 * 1024),
    )(pattern.reshape(-1), blocks)


def solution(mesh):
    return jax.shard_map(
        body,
        mesh=mesh,
        in_specs=(P(("groups", "row", "col"), None, None, None), P(), P("groups")),
        out_specs=P(("groups", "row", "col"), None, None, None),
        check_vma=False,
    )
```

```python
import functools

import jax
import jax.numpy as jnp
from jax import lax
from jax.experimental import pallas as pl
from jax.experimental.pallas import tpu as pltpu
from jax.sharding import PartitionSpec as P

PIECE = 2
AHEAD = 8
LAG = 3
MESH = pl.DeviceIdType.MESH
OWN, PARTNER, ACROSS, ONWARD, FAR = range(5)
SHARDS = 5


def halves(x):
    top = x.astype(jnp.bfloat16)
    return top, (x - top.astype(jnp.float32)).astype(jnp.bfloat16)


def purify_kernel(chips, total, rows, slots, pattern, own, out,
                  held_own, partner, across, onward, far, done, high, low, square, wide, wider,
                  linked, factor, line,
                  load_sem, out_sem, p_send, p_recv, y_send, y_recv, z_send, z_recv, x_send, x_recv):
    width = out.shape[-1]
    held = rows * slots
    pieces = held // PIECE
    per_row = slots // PIECE
    lines = SHARDS * rows
    nothing = SHARDS * held
    chip = lax.axis_index("row")
    core = lax.axis_index("col")
    even = lax.rem(chip, 2) == 0
    step = jnp.where(even, 1, -1)
    paired = {"row": chip + step}
    target = {"row": lax.rem(chip + 2 * step + chips, chips)}
    source = {"row": lax.rem(chip - 2 * step + chips, chips)}
    other = {"col": 1 - core}

    load = pltpu.make_async_copy(own, held_own, load_sem)
    load.start()
    barrier = pltpu.get_barrier_semaphore()
    for device in (paired, target, source, other):
        pl.semaphore_signal(barrier, inc=1, device_id=device, device_id_type=MESH)
    pl.semaphore_wait(barrier, 4)

    def copy(src, dst, send, recv, device):
        return pltpu.make_async_remote_copy(
            src_ref=src, dst_ref=dst, send_sem=send, recv_sem=recv,
            device_id=device, device_id_type=MESH)

    def part(n):
        return pl.ds(n * PIECE, PIECE)

    whole = copy(own, partner, p_send, p_recv, other)
    ys = [copy(own.at[part(n)], across.at[part(n)], y_send.at[n], y_recv.at[n], paired)
          for n in range(pieces)]
    zs = [copy(across.at[part(n)], onward.at[part(n)], z_send.at[n], z_recv.at[n], target)
          for n in range(pieces)]
    xy = [copy(across.at[part(n)], far.at[part(n)], x_send.at[n], x_recv.at[n], other)
          for n in range(pieces)]
    xz = [copy(onward.at[part(n)], far.at[part(n)], x_send.at[n], x_recv.at[n], other)
          for n in range(pieces)]
    from_across = lax.rem(chip, 2) == core

    for n in range(min(AHEAD, pieces)):
        ys[n].start()
    whole.start()

    def split(ref, shard, first, count):
        def one(b, _):
            top, rest = halves(ref[first + b])
            high[shard * held + first + b] = top
            low[shard * held + first + b] = rest
            return 0

        lax.fori_loop(0, count, one, 0)

    def wrapped(x):
        x = jnp.where(x < 0, x + total, x)
        return jnp.where(x >= total, x - total, x)

    mine = (2 * chip + core) * rows
    toward = chip + step
    away = lax.rem(chip - step + chips, chips)
    side = lax.rem(chip - 1 + 2 * core + chips, chips)
    firsts = [mine, (2 * chip + 1 - core) * rows, (2 * toward + core) * rows,
              (2 * away + core) * rows, (2 * side + 1 - core) * rows]

    def tabulate(row, _):
        columns = [pattern[(mine + row) * slots + a] for a in range(slots)]
        places = []
        for a in range(slots):
            place = jnp.int32(0)
            for shard, first in enumerate(firsts):
                off = wrapped(columns[a] - first)
                place = jnp.where(off < rows, shard * rows + off, place)
            line[row * slots + a] = place
            places.append(place)

        def one_line(m, _):
            shard, local = m // rows, m % rows
            at = jnp.int32(0)
            for s, first in enumerate(firsts):
                at = jnp.where(shard == s, first, at)
            at = wrapped(at + local)
            entries = [pattern[at * slots + b] for b in range(slots)]
            slot = jnp.int32(nothing)
            for a in range(slots):
                slot = jnp.where(places[a] == m, row * slots + a, slot)
            factor[row * lines + m] = slot
            for c in range(slots):
                found = jnp.int32(nothing)
                for b in range(slots):
                    found = jnp.where(entries[b] == columns[c], m * slots + b, found)
                linked[(row * lines + m) * slots + c] = found
            return 0

        lax.fori_loop(0, lines, one_line, 0)
        return 0

    def product(left, row, which, c):
        tops, rests = [], []
        for m in which:
            places = [linked[(row * lines + m) * slots + c + k] for k in range(2)]
            tops.append(jnp.concatenate([high[p] for p in places], axis=1))
            rests.append(jnp.concatenate([low[p] for p in places], axis=1))
        both = jnp.dot(left[:, :len(which) * width], jnp.concatenate(tops, axis=0),
                       preferred_element_type=jnp.float32)
        small = jnp.dot(left[:width, :len(which) * width], jnp.concatenate(rests, axis=0),
                        preferred_element_type=jnp.float32)
        return both[:width] + (both[width:] + small)

    def add_lines(which, begin, end, fresh=False):
        def one_row(row, _):
            for t, m in enumerate(which):
                place = factor[row * lines + m]
                wide[:width, t * width:(t + 1) * width] = high[place]
                wide[width:, t * width:(t + 1) * width] = low[place]
            for c in range(0, slots, 2):
                columns = slice(c * width, (c + 2) * width)
                result = product(wide, row, which, c)
                if fresh:
                    square[row, :, columns] = result
                else:
                    square[row, :, columns] += result
            return 0

        lax.fori_loop(begin, end, one_row, 0)

    def remote_lines(r):
        first = [ACROSS] if r == 0 else []
        return [shard * rows + r for shard in first + [ONWARD, FAR]]

    def onward_arrived(n):
        zs[n].wait_recv()

        @pl.when(jnp.logical_not(from_across))
        def _():
            xz[n].start()

        split(onward, ONWARD, n * PIECE, PIECE)

    def far_arrived(n):
        xy[n].wait_recv()
        split(far, FAR, n * PIECE, PIECE)

    jobs = {}
    free = 0

    def then(ready, job, *args):
        nonlocal free
        free = max(ready, free)
        jobs.setdefault(free, []).append((job, args))
        free += 1

    def partner_arrived():
        whole.wait_recv()
        split(partner, PARTNER, 0, held)

    def tables(begin, end):
        lax.fori_loop(begin, end, tabulate, 0)

    for begin in range(0, rows, 2):
        then(0, tables, begin, min(begin + 2, rows))
    then(0, partner_arrived)
    middle = rows // 2
    for begin, end in ((0, middle), (middle, rows)):
        then(0, add_lines, list(range(2 * rows)), begin, end, True)
    for r in range(rows - 1):
        group = remote_lines(r) + [ACROSS * rows + r + 1]
        for begin, end in ((0, middle), (middle, rows)):
            then((r + 2) * per_row - 1, add_lines, group, begin, end)

    high[nothing] = jnp.zeros((width, width), jnp.bfloat16)
    low[nothing] = jnp.zeros((width, width), jnp.bfloat16)
    load.wait()
    split(held_own, OWN, 0, held)
    for n in range(pieces + LAG + 1):
        if n < pieces:
            ys[n].wait_recv()
            zs[n].start()

            @pl.when(from_across)
            def _():
                xy[n].start()

            if n + AHEAD < pieces:
                ys[n].wait_send()
                ys[n + AHEAD].start()
            split(across, ACROSS, n * PIECE, PIECE)
        if LAG <= n < pieces + LAG:
            onward_arrived(n - LAG)
        if n >= LAG + 1:
            far_arrived(n - LAG - 1)
        for job, args in jobs.pop(n, []):
            job(*args)
    for n in sorted(jobs):
        for job, args in jobs[n]:
            job(*args)
    add_lines(remote_lines(rows - 1), 0, rows)

    def leave(row):
        return pltpu.make_async_copy(done.at[row], out.at[row], out_sem.at[row])

    def finish(row, _):
        for c in range(0, slots, 2):
            columns = slice(c * width, (c + 2) * width)
            top, rest = halves(square[row, :, columns])
            wider[:width, columns] = top
            wider[width:, columns] = rest
        which = [line[row * slots + a] for a in range(slots)]
        for c in range(0, slots, 2):
            columns = slice(c * width, (c + 2) * width)
            result = 1.5 * square[row, :, columns] - product(wider, row, which, c)
            done[row, c] = result[:, :width]
            done[row, c + 1] = result[:, width:]
        leave(row).start()
        return 0

    lax.fori_loop(0, rows, finish, 0)
    for n in range(pieces):
        if n + AHEAD >= pieces:
            ys[n].wait_send()
        zs[n].wait_send()
        xy[n].wait_send()
    whole.wait_send()
    for row in range(rows):
        leave(row).wait()


def body(density, pattern_table, structure_id):
    rows, slots, width, _ = density.shape
    total = pattern_table.shape[1]
    held = rows * slots
    pieces = held // PIECE
    pattern = lax.dynamic_index_in_dim(pattern_table, structure_id[0], 0, keepdims=False)
    blocks = density.reshape(held, width, width)
    dma, vmem, smem, narrow = pltpu.SemaphoreType.DMA, pltpu.VMEM, pltpu.SMEM, jnp.bfloat16
    lines = SHARDS * rows
    halved = pl.pallas_call(
        functools.partial(purify_kernel, lax.axis_size("row"), total, rows, slots),
        out_shape=jax.ShapeDtypeStruct(density.shape, density.dtype),
        in_specs=[pl.BlockSpec(memory_space=smem), pl.BlockSpec(memory_space=pl.ANY)],
        out_specs=pl.BlockSpec(memory_space=pl.ANY),
        scratch_shapes=[vmem(blocks.shape, blocks.dtype)] * 5
        + [vmem(density.shape, density.dtype)]
        + [vmem((SHARDS * held + 1, width, width), narrow)] * 2
        + [
            vmem((rows, width, slots * width), jnp.float32),
            vmem((2 * width, 2 * rows * width), narrow),
            vmem((2 * width, slots * width), narrow),
            smem((rows * lines * slots,), jnp.int32),
            smem((rows * lines,), jnp.int32),
            smem((rows * slots,), jnp.int32),
            dma, dma((rows,)), dma, dma,
        ] + [dma((pieces,))] * 6,
        compiler_params=pltpu.CompilerParams(
            collective_id=0, has_side_effects=True, vmem_limit_bytes=56 * 1024 * 1024),
    )(pattern.reshape(-1), blocks)
    return 2.0 * halved


def solution(mesh):
    return jax.shard_map(
        body,
        mesh=mesh,
        in_specs=(P(("groups", "row", "col"), None, None, None), P(), P("groups")),
        out_specs=P(("groups", "row", "col"), None, None, None),
        check_vma=False,
    )
```
